32 devices in a mesh: groups: 2 (over y), rows: 4 (over z), cols: 2 (over x), sub: 2 (over core).
Axes of the slice: x: 2, y: 2, z: 4, core: 2. Of those that a mesh axis runs over, the one named last changes fastest.
Arguments:
- scf_blocks: bfloat16 [4096, 128, 128], P(('groups', 'rows', 'cols', 'sub')), parts along dimension 0, may hold values from -0.125 to 0.125
- scf_source: int32 [256, 16], P(('groups', 'rows', 'sub'), 'cols'), parts along dimension 0, may hold values from 0 to 127, as said below
- pattern: int32 [256, 16], P(('groups', 'rows', 'sub'), 'cols'), parts along dimension 0, may hold values from 0 to 127, as said below
- panel: bfloat16 [32768, 128], P(('groups', 'rows', 'sub')), parts along dimension 0, may hold values from -6 to 6
Outputs:
- cheb_one: bfloat16 [32768, 128], P(('groups', 'rows', 'sub')), parts along dimension 0
- cheb_two: bfloat16 [32768, 128], P(('groups', 'rows', 'sub')), parts along dimension 0
The draws below stay inside these ranges and needn't reach their ends.
There are 2 independent parts, one for each index of `groups`. The reference program is written for one: setup_inputs(seed, part) draws one part's arguments, and reference() takes and returns one part's arrays. A program takes and returns all parts, laid end to end along the dimension named above; each array names one. Nothing has to cross between parts.
Inputs may be any that keep to these rules, and one draw needn't show every extreme that they name: `pattern`: the 16 block columns of each block row are distinct, each within 16 blocks of the row's own index counted cyclically over the 128 block rows, and every block row has one at offset 0, one at -16 and one at +16. `scf_source`: each device's tile of 16 x 8 entries is a permutation of 0 to 127.
All inputs are finite; a program needn't handle non-finite values.
Results may differ from the reference program's by a relative error of at most 0.0046.
Values may be sent and summed in bfloat16 or wider, within the bound.
A program may use at most 64 MiB of HBM per device.

```python
import jax
import jax.numpy as jnp
from jax import lax

BS = 128
PC = 128
KB = 16
BR_DEV = 16
KB_COL = 8
SLOTS = 128
NB = 128
ROWS = 16384
N_ROWS = 4
N_COLS = 2
N_SUB = 2


def draw_pattern(key, part):
    reach = BR_DEV
    span = 2 * reach + 1
    key_one = jax.random.fold_in(key, 11)
    key_two = jax.random.fold_in(key, 12)
    offsets = jnp.arange(span, dtype=jnp.int32) - reach
    scores = jax.random.randint(key_one, (NB, span), 0, 2 ** 16, dtype=jnp.int32) * span + jnp.arange(span, dtype=jnp.int32)[None, :]
    forced = ((offsets == 0) | (offsets == reach) | (offsets == -reach)).astype(jnp.int32)
    scores = scores + forced[None, :] * 2 ** 28
    unused, chosen = lax.top_k(scores, KB)
    mixing = jax.random.randint(key_two, (NB, KB), 0, 2 ** 16, dtype=jnp.int32) * KB + jnp.arange(KB, dtype=jnp.int32)[None, :]
    order_cols = jnp.argsort(mixing, axis=1, stable=True)
    chosen = jnp.take_along_axis(chosen, order_cols, axis=1)
    row_ids = jnp.arange(NB, dtype=jnp.int32)[:, None]
    return ((row_ids + chosen - reach + NB) % NB).astype(jnp.int32)


def draw_scf_source(key, part):
    count_rows = NB // BR_DEV
    count_cols = KB // KB_COL
    key_one = jax.random.fold_in(key, 21)
    scores = jax.random.randint(key_one, (count_rows, count_cols, SLOTS), 0, 2 ** 16, dtype=jnp.int32) * SLOTS + jnp.arange(SLOTS, dtype=jnp.int32)
    perms = jnp.argsort(scores, axis=-1, stable=True).astype(jnp.int32)
    perms = perms.reshape(count_rows, count_cols, BR_DEV, KB_COL)
    return jnp.transpose(perms, (0, 2, 1, 3)).reshape(NB, KB).astype(jnp.int32)


def levels(rng, extent, shards, low, largest):
    loudness = 1.0
    for axis_at, parts in shards:
        draws = jax.random.uniform(jax.random.fold_in(jax.random.fold_in(rng, 6), axis_at), (parts,), jnp.float32, low / len(shards), largest / len(shards))
        loudness = loudness * jnp.repeat(jnp.exp(draws), extent[axis_at] // parts).reshape((-1,) + (1,) * (len(extent) - 1 - axis_at))
    return loudness


def gaussian(stream_key, dims, width, most, shards=(), held_as=jnp.bfloat16):
    entries = jax.random.normal(stream_key, dims, jnp.float32) * width
    if len(shards) > 0:
        entries = levels(stream_key, dims, shards, -0.22, 0.18) * entries
    return jnp.clip(entries, min=-most, max=most).astype(held_as)


def setup_inputs(seed: int = 0, part: int = 0) -> dict:
    key_list = jax.random.split(jax.random.key(seed), 5)
    own_keys = jax.random.split(jax.random.fold_in(key_list[4], part), 5)
    scf_blocks = gaussian(own_keys[0], (NB * KB, BS, BS), (KB * BS) ** -0.5, 0.125, ((0, 16),))
    scf_source = draw_scf_source(jax.random.fold_in(jax.random.fold_in(key_list[4], part), 71), part)
    pattern = draw_pattern(jax.random.fold_in(jax.random.fold_in(key_list[4], part), 71), part)
    panel = gaussian(own_keys[3], (ROWS, PC), 1.0, 6.0, ((0, 8),))
    return {"scf_blocks": scf_blocks, "scf_source": scf_source, "pattern": pattern, "panel": panel}


def reference(scf_blocks, scf_source, pattern, panel):
    per_pair = SLOTS // (N_ROWS * N_SUB)
    row_ids = jnp.arange(NB, dtype=jnp.int32)[:, None]
    slot_ids = jnp.arange(KB, dtype=jnp.int32)[None, :]
    owner = row_ids // BR_DEV
    owner_col = slot_ids // KB_COL
    source_dev = scf_source // per_pair
    source_pos = scf_source % per_pair
    source_row = source_dev // N_SUB
    source_sub = source_dev % N_SUB
    block_ids = (((source_row * N_COLS + owner_col) * N_SUB + source_sub) * SLOTS + owner * per_pair + source_pos).astype(jnp.int32)

    def apply_ham(operand):
        tile_stack = operand.reshape(NB, BS, PC)

        def one_row(inputs):
            ids_row, cols_row = inputs
            chosen = scf_blocks[ids_row].astype(jnp.float32)
            picked = tile_stack[cols_row].astype(jnp.float32)
            return jnp.einsum("kij,kjc->ic", chosen, picked)

        result = lax.map(one_row, (block_ids, pattern.astype(jnp.int32)), batch_size=16)
        return result.reshape(NB * BS, PC)

    first = apply_ham(panel)
    cheb_one = first.astype(jnp.bfloat16)
    second = 2.0 * apply_ham(cheb_one) - panel.astype(jnp.float32)
    return cheb_one, second.astype(jnp.bfloat16)
```

```python
import jax
import jax.numpy as jnp
from jax import lax
from jax.experimental import pallas as pl
from jax.experimental.pallas import tpu as pltpu
from jax.sharding import PartitionSpec as P

MESH = pl.DeviceIdType.MESH


def kernel(
    blocks_ref, panel_ref, order_ref, cols_ref, one_ref, two_ref,
    recv, ext_one, ext_two, parts_one, parts_two,
    own_sem, block_send, block_recv, halo_send, halo_recv,
    next_send, next_recv, one_send, one_recv, two_send, two_recv,
):
    slots = blocks_ref.shape[0]
    br_dev = panel_ref.shape[0]
    kb_col = cols_ref.shape[0] // br_dev
    count_rows = lax.axis_size("rows")
    count_sub = lax.axis_size("sub")
    count_cols = lax.axis_size("cols")
    owners = count_rows * count_sub
    per_pair = slots // owners
    me = lax.axis_index("rows") * count_sub + lax.axis_index("sub")
    my_col = lax.axis_index("cols")

    def owner_id(owner):
        return {"rows": owner // count_sub, "sub": owner % count_sub}

    def col_id(hop):
        return {"cols": (my_col + hop) % count_cols}

    barrier = pltpu.get_barrier_semaphore()

    @pl.loop(1, owners)
    def _(hop):
        pl.semaphore_signal(barrier, inc=1, device_id=owner_id((me + hop) % owners), device_id_type=MESH)

    @pl.loop(1, count_cols)
    def _(hop):
        pl.semaphore_signal(barrier, inc=1, device_id=col_id(hop), device_id_type=MESH)

    pl.semaphore_wait(barrier, owners - 1 + count_cols - 1)

    right = (me + 1) % owners
    left = (me + owners - 1) % owners

    def block_copy(hop):
        target = (me + hop) % owners
        return pltpu.make_async_remote_copy(
            src_ref=blocks_ref.at[pl.ds(target * per_pair, per_pair)],
            dst_ref=recv.at[pl.ds(me * per_pair, per_pair)],
            send_sem=block_send.at[hop],
            recv_sem=block_recv.at[hop],
            device_id=owner_id(target),
            device_id_type=MESH,
        )

    def halo_copy(side):
        return pltpu.make_async_remote_copy(
            src_ref=panel_ref,
            dst_ref=ext_one.at[pl.ds(0 if side == 0 else 2 * br_dev, br_dev)],
            send_sem=halo_send.at[side],
            recv_sem=halo_recv.at[side],
            device_id=owner_id(right if side == 0 else left),
            device_id_type=MESH,
        )

    own_blocks = pltpu.make_async_copy(
        blocks_ref.at[pl.ds(me * per_pair, per_pair)],
        recv.at[pl.ds(me * per_pair, per_pair)],
        own_sem.at[0],
    )
    own_panel = pltpu.make_async_copy(panel_ref, ext_one.at[pl.ds(br_dev, br_dev)], own_sem.at[1])

    @pl.loop(1, owners)
    def _(step):
        half = owners // 2
        hop = (half + jnp.where(step % 2 == 0, step // 2, owners - step // 2)) % owners
        block_copy(hop).start()

    for side in (0, 1):
        halo_copy(side).start()
    own_blocks.start()
    own_panel.start()
    own_blocks.wait()
    own_panel.wait()
    for side in (0, 1):
        halo_copy(side).wait()

    @pl.loop(1, owners)
    def _(hop):
        block_copy(hop).wait()

    def row_copy(parts, send, receive, row, hop):
        return pltpu.make_async_remote_copy(
            src_ref=parts.at[my_col, row],
            dst_ref=parts.at[my_col, row],
            send_sem=send.at[row, hop],
            recv_sem=receive.at[row, hop],
            device_id=col_id(hop),
            device_id_type=MESH,
        )

    def multiply(ext, parts, send, receive):
        @pl.loop(0, br_dev)
        def _(row):
            base = row * kb_col
            lhs = jnp.concatenate([recv[order_ref[base + k]] for k in range(kb_col)], axis=1)
            rhs = jnp.concatenate([ext[cols_ref[base + k]] for k in range(kb_col)], axis=0)
            parts[my_col, row] = jnp.dot(lhs, rhs, preferred_element_type=jnp.float32)
            for hop in range(1, count_cols):
                row_copy(parts, send, receive, row, hop).start()

    def summed(parts, send, receive, row):
        for hop in range(1, count_cols):
            row_copy(parts, send, receive, row, hop).wait()
        total = parts[0, row]
        for col in range(1, count_cols):
            total = total + parts[col, row]
        return total

    def next_copy(row, side):
        return pltpu.make_async_remote_copy(
            src_ref=ext_two.at[br_dev + row],
            dst_ref=ext_two.at[row if side == 0 else 2 * br_dev + row],
            send_sem=next_send.at[row, side],
            recv_sem=next_recv.at[row, side],
            device_id=owner_id(right if side == 0 else left),
            device_id_type=MESH,
        )

    multiply(ext_one, parts_one, one_send, one_recv)

    @pl.loop(0, br_dev)
    def _(row):
        value = summed(parts_one, one_send, one_recv, row).astype(jnp.bfloat16)
        ext_two[br_dev + row] = value
        for side in (0, 1):
            next_copy(row, side).start()
        one_ref[row] = value

    @pl.loop(0, br_dev)
    def _(row):
        for side in (0, 1):
            next_copy(row, side).wait()

    multiply(ext_two, parts_two, two_send, two_recv)

    @pl.loop(0, br_dev)
    def _(row):
        total = summed(parts_two, two_send, two_recv, row)
        two_ref[row] = (2.0 * total - ext_one[br_dev + row].astype(jnp.float32)).astype(jnp.bfloat16)


def local(scf_blocks, scf_source, pattern, panel):
    br_dev, kb_col = pattern.shape
    slots, block_len, _ = scf_blocks.shape
    width = panel.shape[1]
    count_cols = lax.axis_size("cols")
    owners = lax.axis_size("rows") * lax.axis_size("sub")
    tiles = br_dev * owners
    me = lax.axis_index("rows") * lax.axis_size("sub") + lax.axis_index("sub")
    local_cols = ((pattern - (me - 1) * br_dev + tiles) % tiles).reshape(-1)
    order = scf_source.reshape(-1)
    tile = (block_len, width)
    out = jax.ShapeDtypeStruct((br_dev, *tile), jnp.bfloat16)
    vmem = pl.BlockSpec(memory_space=pltpu.VMEM)
    smem = pl.BlockSpec(memory_space=pltpu.SMEM)
    hbm = pl.BlockSpec(memory_space=pl.ANY)
    dma = pltpu.SemaphoreType.DMA
    one, two = pl.pallas_call(
        kernel,
        out_shape=(out, out),
        in_specs=[hbm, hbm, smem, smem],
        out_specs=(vmem, vmem),
        scratch_shapes=[
            pltpu.VMEM((slots, block_len, block_len), jnp.bfloat16),
            pltpu.VMEM((3 * br_dev, *tile), jnp.bfloat16),
            pltpu.VMEM((3 * br_dev, *tile), jnp.bfloat16),
            pltpu.VMEM((count_cols, br_dev, *tile), jnp.float32),
            pltpu.VMEM((count_cols, br_dev, *tile), jnp.float32),
            dma((2,)),
            dma((owners,)),
            dma((owners,)),
            dma((2,)),
            dma((2,)),
            dma((br_dev, 2)),
            dma((br_dev, 2)),
            dma((br_dev, count_cols)),
            dma((br_dev, count_cols)),
            dma((br_dev, count_cols)),
            dma((br_dev, count_cols)),
        ],
        compiler_params=pltpu.CompilerParams(
            collective_id=0, has_side_effects=True, vmem_limit_bytes=32 * 2**20
        ),
    )(scf_blocks, panel.reshape(br_dev, *tile), order, local_cols)
    return one.reshape(panel.shape), two.reshape(panel.shape)


def solution(mesh):
    return jax.shard_map(
        local,
        mesh=mesh,
        in_specs=(
            P(("groups", "rows", "cols", "sub"), None, None),
            P(("groups", "rows", "sub"), "cols"),
            P(("groups", "rows", "sub"), "cols"),
            P(("groups", "rows", "sub"), None),
        ),
        out_specs=(P(("groups", "rows", "sub"), None), P(("groups", "rows", "sub"), None)),
        check_vma=False,
    )
```

```python
import jax
import jax.numpy as jnp
from jax import lax
from jax.experimental import pallas as pl
from jax.experimental.pallas import tpu as pltpu
from jax.sharding import PartitionSpec as P

MESH = pl.DeviceIdType.MESH
SEND = jnp.bfloat16
VMEM_MIB = 32


def kernel(
    blocks_ref, panel_ref, order_ref, pattern_ref, one_ref, two_ref,
    recv, ext_one, ext_two, outbox, inbox, own, final,
    own_sem, block_send, block_recv, halo_send, halo_recv, pass_send, pass_recv,
    next_send, next_recv, sum_send, sum_recv, share_send, share_recv,
):
    slots = blocks_ref.shape[0]
    br_dev, kb_col = pattern_ref.shape
    count_sub = lax.axis_size("sub")
    count_cols = lax.axis_size("cols")
    owners = lax.axis_size("rows") * count_sub
    per_pair = slots // owners
    chunk = br_dev // count_cols
    tiles = owners * br_dev
    me = lax.axis_index("rows") * count_sub + lax.axis_index("sub")
    my_col = lax.axis_index("cols")
    right = (me + 1) % owners
    left = (me + owners - 1) % owners
    col_hops = range(1, count_cols)
    bases = (0, 2 * br_dev)

    def owner_id(owner):
        return {"rows": owner // count_sub, "sub": owner % count_sub}

    def col_id(hop):
        return {"cols": (my_col + hop) % count_cols}

    def remote(src, dst, send_sem, recv_sem, device_id):
        return pltpu.make_async_remote_copy(
            src_ref=src, dst_ref=dst, send_sem=send_sem, recv_sem=recv_sem,
            device_id=device_id, device_id_type=MESH,
        )

    barrier = pltpu.get_barrier_semaphore()

    @pl.loop(1, owners)
    def _(hop):
        pl.semaphore_signal(barrier, inc=1, device_id=owner_id((me + hop) % owners), device_id_type=MESH)

    for hop in col_hops:
        pl.semaphore_signal(barrier, inc=1, device_id=col_id(hop), device_id_type=MESH)
    pl.semaphore_wait(barrier, owners - 1 + count_cols - 1)

    def block_copy(target, slot):
        return remote(
            blocks_ref.at[pl.ds(target * per_pair, per_pair)],
            recv.at[pl.ds(me * per_pair, per_pair)],
            block_send.at[slot], block_recv.at[slot], owner_id(target),
        )

    def halo_copy(side):
        return remote(
            panel_ref.at[pl.ds(my_col * chunk, chunk)],
            ext_one.at[pl.ds(bases[side] + my_col * chunk, chunk)],
            halo_send.at[side], halo_recv.at[side], owner_id((right, left)[side]),
        )

    def pass_copy(side, hop):
        part = ext_one.at[pl.ds(bases[side] + my_col * chunk, chunk)]
        return remote(part, part, pass_send.at[side, hop], pass_recv.at[side, hop], col_id(hop))

    own_blocks = pltpu.make_async_copy(
        blocks_ref.at[pl.ds(me * per_pair, per_pair)],
        recv.at[pl.ds(me * per_pair, per_pair)],
        own_sem.at[0],
    )
    own_panel = pltpu.make_async_copy(panel_ref, ext_one.at[pl.ds(br_dev, br_dev)], own_sem.at[1])

    for side in (0, 1):
        halo_copy(side).start()

    if owners & (owners - 1):
        @pl.loop(1, owners)
        def _(hop):
            block_copy((me + hop) % owners, hop).start()
    else:
        half = owners // 2
        while half:
            base = me // (2 * half) * (2 * half)
            sibling = base + (1 - (me - base) // half) * half

            @pl.loop(0, half)
            def _(step, half=half, sibling=sibling):
                block_copy(sibling + (me + step) % half, half + step).start()

            half //= 2

    own_blocks.start()
    own_panel.start()
    for side in (0, 1):
        halo_copy(side).wait()
        for hop in col_hops:
            pass_copy(side, hop).start()
    own_blocks.wait()
    own_panel.wait()
    for side in (0, 1):
        for hop in col_hops:
            pass_copy(side, hop).wait()

    @pl.loop(1, owners)
    def _(slot):
        block_copy((me + slot) % owners, slot).wait()

    first_tile = (me - 1) * br_dev

    def product(ext, row):
        lhs, rhs = [], []
        for k in range(kb_col):
            tile = pattern_ref[row, k] - first_tile
            tile = jnp.where(tile < 0, tile + tiles, tile)
            tile = jnp.where(tile >= tiles, tile - tiles, tile)
            tile = jnp.minimum(tile, 3 * br_dev - 1)
            lhs.append(recv[order_ref[row, k]])
            rhs.append(ext[tile])
        return jnp.dot(
            jnp.concatenate(lhs, axis=1), jnp.concatenate(rhs, axis=0),
            preferred_element_type=jnp.float32,
        )

    def sum_copy(turn, hop, step):
        row = (my_col + hop) % count_cols * chunk + step
        return remote(
            outbox.at[turn, row], inbox.at[turn, hop, step],
            sum_send.at[turn, hop, step], sum_recv.at[turn, hop, step], col_id(hop),
        )

    def multiply(ext, turn):
        for hop in col_hops:
            @pl.loop(0, chunk)
            def _(step, hop=hop):
                row = (my_col + hop) % count_cols * chunk + step
                outbox[turn, row] = product(ext, row).astype(SEND)
                sum_copy(turn, hop, step).start()

        @pl.loop(0, chunk)
        def _(step):
            own[step] = product(ext, my_col * chunk + step)

    def summed(turn, step):
        total = own[step]
        for hop in col_hops:
            sum_copy(turn, hop, step).wait()
            total = total + inbox[turn, hop, step].astype(jnp.float32)
        return total

    def share_copy(turn, ref, base, hop, step):
        part = ref.at[base + my_col * chunk + step]
        return remote(
            part, part, share_send.at[turn, hop, step], share_recv.at[turn, hop, step], col_id(hop)
        )

    def next_copy(row, side):
        return remote(
            ext_two.at[br_dev + row], ext_two.at[bases[side] + row],
            next_send.at[row, side], next_recv.at[row, side], owner_id((right, left)[side]),
        )

    multiply(ext_one, 0)

    @pl.loop(0, chunk)
    def _(step):
        row = my_col * chunk + step
        ext_two[br_dev + row] = summed(0, step).astype(jnp.bfloat16)
        for hop in col_hops:
            share_copy(0, ext_two, br_dev, hop, step).start()
        for side in (0, 1):
            next_copy(row, side).start()

    for hop in col_hops:
        @pl.loop(0, chunk)
        def _(step, hop=hop):
            share_copy(0, ext_two, br_dev, hop, step).wait()
            row = (my_col + count_cols - hop) % count_cols * chunk + step
            for side in (0, 1):
                next_copy(row, side).start()

    out_one = pltpu.make_async_copy(ext_two.at[pl.ds(br_dev, br_dev)], one_ref, own_sem.at[2])
    out_one.start()

    @pl.loop(0, br_dev)
    def _(row):
        for side in (0, 1):
            next_copy(row, side).wait()

    multiply(ext_two, 1)

    @pl.loop(0, chunk)
    def _(step):
        row = my_col * chunk + step
        total = 2.0 * summed(1, step) - ext_one[br_dev + row].astype(jnp.float32)
        final[row] = total.astype(jnp.bfloat16)
        for hop in col_hops:
            share_copy(1, final, 0, hop, step).start()

    for hop in col_hops:
        @pl.loop(0, chunk)
        def _(step, hop=hop):
            share_copy(1, final, 0, hop, step).wait()

    out_two = pltpu.make_async_copy(final, two_ref, own_sem.at[3])
    out_two.start()
    out_one.wait()
    out_two.wait()


def local(scf_blocks, scf_source, pattern, panel):
    br_dev, kb_col = pattern.shape
    slots, block_len, _ = scf_blocks.shape
    tile = (block_len, panel.shape[1])
    count_cols = lax.axis_size("cols")
    owners = lax.axis_size("rows") * lax.axis_size("sub")
    chunk = br_dev // count_cols
    out = jax.ShapeDtypeStruct((br_dev, *tile), jnp.bfloat16)
    smem = pl.BlockSpec(memory_space=pltpu.SMEM)
    hbm = pl.BlockSpec(memory_space=pl.ANY)
    dma = pltpu.SemaphoreType.DMA
    one, two = pl.pallas_call(
        kernel,
        out_shape=(out, out),
        in_specs=[hbm, hbm, smem, smem],
        out_specs=(hbm, hbm),
        scratch_shapes=[
            pltpu.VMEM((slots, block_len, block_len), jnp.bfloat16),
            pltpu.VMEM((3 * br_dev, *tile), jnp.bfloat16),
            pltpu.VMEM((3 * br_dev, *tile), jnp.bfloat16),
            pltpu.VMEM((2, br_dev, *tile), SEND),
            pltpu.VMEM((2, count_cols, chunk, *tile), SEND),
            pltpu.VMEM((chunk, *tile), jnp.float32),
            pltpu.VMEM((br_dev, *tile), jnp.bfloat16),
            dma((4,)),
            dma((owners,)),
            dma((owners,)),
            dma((2,)),
            dma((2,)),
            dma((2, count_cols)),
            dma((2, count_cols)),
            dma((br_dev, 2)),
            dma((br_dev, 2)),
            dma((2, count_cols, chunk)),
            dma((2, count_cols, chunk)),
            dma((2, count_cols, chunk)),
            dma((2, count_cols, chunk)),
        ],
        compiler_params=pltpu.CompilerParams(
            collective_id=0, has_side_effects=True, vmem_limit_bytes=VMEM_MIB * 2**20
        ),
    )(scf_blocks, panel.reshape(br_dev, *tile), scf_source, pattern)
    return one.reshape(panel.shape), two.reshape(panel.shape)


def solution(mesh):
    return jax.shard_map(
        local,
        mesh=mesh,
        in_specs=(
            P(("groups", "rows", "cols", "sub"), None, None),
            P(("groups", "rows", "sub"), "cols"),
            P(("groups", "rows", "sub"), "cols"),
            P(("groups", "rows", "sub"), None),
        ),
        out_specs=(P(("groups", "rows", "sub"), None), P(("groups", "rows", "sub"), None)),
        check_vma=False,
    )
```

```python
import jax
import jax.numpy as jnp
from jax import lax
from jax.experimental import pallas as pl
from jax.experimental.pallas import tpu as pltpu
from jax.sharding import PartitionSpec as P

MESH = pl.DeviceIdType.MESH
SEND = jnp.bfloat16
VMEM_MIB = 32


def kernel(
    blocks_ref, panel_ref, order_ref, pattern_ref, one_ref, two_ref,
    recv, ext_one, ext_two, outbox, inbox, own, final,
    own_sem, block_send, block_recv, halo_send, halo_recv, pass_send, pass_recv,
    next_send, next_recv, sum_send, sum_recv, share_send, share_recv,
):
    slots = blocks_ref.shape[0]
    br_dev, kb_col = pattern_ref.shape
    count_sub = lax.axis_size("sub")
    count_cols = lax.axis_size("cols")
    owners = lax.axis_size("rows") * count_sub
    per_pair = slots // owners
    chunk = br_dev // count_cols
    tiles = owners * br_dev
    me = lax.axis_index("rows") * count_sub + lax.axis_index("sub")
    my_col = lax.axis_index("cols")
    right = (me + 1) % owners
    left = (me + owners - 1) % owners
    col_hops = range(1, count_cols)
    bases = (0, 2 * br_dev)

    def owner_id(owner):
        return {"rows": owner // count_sub, "sub": owner % count_sub}

    def col_id(hop):
        return {"cols": (my_col + hop) % count_cols}

    def remote(src, dst, send_sem, recv_sem, device_id):
        return pltpu.make_async_remote_copy(
            src_ref=src, dst_ref=dst, send_sem=send_sem, recv_sem=recv_sem,
            device_id=device_id, device_id_type=MESH,
        )

    barrier = pltpu.get_barrier_semaphore()

    def block_copy(target, slot):
        return remote(
            blocks_ref.at[pl.ds(target * per_pair, per_pair)],
            recv.at[pl.ds(me * per_pair, per_pair)],
            block_send.at[slot], block_recv.at[slot], owner_id(target),
        )

    middle = lax.axis_size("rows") // 2
    early = 2 * count_sub
    late = owners - early
    first_early = (middle - 1) * count_sub
    first_late = first_early + early
    my_row = lax.axis_index("rows")
    is_early = (my_row == middle) | (my_row == middle - 1)
    facing = 2 * middle - 1 - my_row

    def greet(owner):
        pl.semaphore_signal(barrier, inc=1, device_id=owner_id(owner), device_id_type=MESH)

    def greet_cols():
        for hop in col_hops:
            pl.semaphore_signal(barrier, inc=1, device_id=col_id(hop), device_id_type=MESH)

    @pl.when(is_early)
    def _():
        @pl.loop(1, early)
        def _(hop):
            greet(first_early + (me - first_early + hop) % early)

        greet_cols()
        pl.semaphore_wait(barrier, early - 1 + count_cols - 1)

        @pl.loop(0, count_sub)
        def _(step):
            half = owners // 2
            target = facing * count_sub + step
            block_copy(target, half + (target - me + owners) % half).start()

        @pl.loop(0, late)
        def _(step):
            greet((first_late + step) % owners)

        pl.semaphore_wait(barrier, late)

    @pl.when(jnp.logical_not(is_early))
    def _():
        place = (me + owners - first_late) % owners

        @pl.loop(1, late)
        def _(hop):
            greet((first_late + (place + hop) % late) % owners)

        greet_cols()
        pl.semaphore_wait(barrier, owners - 1 + count_cols - 1)

        @pl.loop(0, early)
        def _(step):
            greet(first_early + step)

    def halo_copy(side):
        return remote(
            panel_ref.at[pl.ds(my_col * chunk, chunk)],
            ext_one.at[pl.ds(bases[side] + my_col * chunk, chunk)],
            halo_send.at[side], halo_recv.at[side], owner_id((right, left)[side]),
        )

    def pass_copy(side, hop):
        part = ext_one.at[pl.ds(bases[side] + my_col * chunk, chunk)]
        return remote(part, part, pass_send.at[side, hop], pass_recv.at[side, hop], col_id(hop))

    own_blocks = pltpu.make_async_copy(
        blocks_ref.at[pl.ds(me * per_pair, per_pair)],
        recv.at[pl.ds(me * per_pair, per_pair)],
        own_sem.at[0],
    )
    own_panel = pltpu.make_async_copy(panel_ref, ext_one.at[pl.ds(br_dev, br_dev)], own_sem.at[1])

    for side in (0, 1):
        halo_copy(side).start()

    half = owners // 2
    while half:
        base = me // (2 * half) * (2 * half)
        sibling = base + (1 - (me - base) // half) * half

        @pl.loop(0, half)
        def _(step, half=half, sibling=sibling):
            target = sibling + (me + step) % half
            if half == owners // 2:
                @pl.when(jnp.logical_not(is_early & (target // count_sub == facing)))
                def _():
                    block_copy(target, half + step).start()
            else:
                block_copy(target, half + step).start()

        half //= 2

    own_blocks.start()
    own_panel.start()
    for side in (0, 1):
        halo_copy(side).wait()
        for hop in col_hops:
            pass_copy(side, hop).start()
    own_blocks.wait()
    own_panel.wait()
    for side in (0, 1):
        for hop in col_hops:
            pass_copy(side, hop).wait()

    @pl.loop(1, owners)
    def _(slot):
        block_copy((me + slot) % owners, slot).wait()

    first_tile = (me - 1) * br_dev

    def product(ext, row):
        lhs, rhs = [], []
        for k in range(kb_col):
            tile = pattern_ref[row, k] - first_tile
            tile = jnp.where(tile < 0, tile + tiles, tile)
            tile = jnp.where(tile >= tiles, tile - tiles, tile)
            tile = jnp.minimum(tile, 3 * br_dev - 1)
            lhs.append(recv[order_ref[row, k]])
            rhs.append(ext[tile])
        return jnp.dot(
            jnp.concatenate(lhs, axis=1), jnp.concatenate(rhs, axis=0),
            preferred_element_type=jnp.float32,
        )

    def sum_copy(turn, hop, step):
        row = (my_col + hop) % count_cols * chunk + step
        return remote(
            outbox.at[turn, row], inbox.at[turn, hop, step],
            sum_send.at[turn, hop, step], sum_recv.at[turn, hop, step], col_id(hop),
        )

    def multiply(ext, turn):
        for hop in col_hops:
            @pl.loop(0, chunk, unroll=chunk)
            def _(step, hop=hop):
                row = (my_col + hop) % count_cols * chunk + step
                outbox[turn, row] = product(ext, row).astype(SEND)
                sum_copy(turn, hop, step).start()

        @pl.loop(0, chunk, unroll=chunk)
        def _(step):
            own[step] = product(ext, my_col * chunk + step)

    def summed(turn, step):
        total = own[step]
        for hop in col_hops:
            sum_copy(turn, hop, step).wait()
            total = total + inbox[turn, hop, step].astype(jnp.float32)
        return total

    def share_copy(turn, ref, base, hop, step):
        part = ref.at[base + my_col * chunk + step]
        return remote(
            part, part, share_send.at[turn, hop, step], share_recv.at[turn, hop, step], col_id(hop)
        )

    def next_copy(row, side):
        return remote(
            ext_two.at[br_dev + row], ext_two.at[bases[side] + row],
            next_send.at[row, side], next_recv.at[row, side], owner_id((right, left)[side]),
        )

    multiply(ext_one, 0)

    @pl.loop(0, chunk)
    def _(step):
        row = my_col * chunk + step
        ext_two[br_dev + row] = summed(0, step).astype(jnp.bfloat16)
        for hop in col_hops:
            share_copy(0, ext_two, br_dev, hop, step).start()
        for side in (0, 1):
            next_copy(row, side).start()

    for hop in col_hops:
        @pl.loop(0, chunk)
        def _(step, hop=hop):
            share_copy(0, ext_two, br_dev, hop, step).wait()
            row = (my_col + count_cols - hop) % count_cols * chunk + step
            for side in (0, 1):
                next_copy(row, side).start()

    out_one = pltpu.make_async_copy(ext_two.at[pl.ds(br_dev, br_dev)], one_ref, own_sem.at[2])
    out_one.start()

    @pl.loop(0, br_dev)
    def _(row):
        for side in (0, 1):
            next_copy(row, side).wait()

    multiply(ext_two, 1)

    @pl.loop(0, chunk)
    def _(step):
        row = my_col * chunk + step
        total = 2.0 * summed(1, step) - ext_one[br_dev + row].astype(jnp.float32)
        final[row] = total.astype(jnp.bfloat16)
        for hop in col_hops:
            share_copy(1, final, 0, hop, step).start()

    for hop in col_hops:
        @pl.loop(0, chunk)
        def _(step, hop=hop):
            share_copy(1, final, 0, hop, step).wait()

    out_two = pltpu.make_async_copy(final, two_ref, own_sem.at[3])
    out_two.start()
    out_one.wait()
    out_two.wait()


def local(scf_blocks, scf_source, pattern, panel):
    br_dev, kb_col = pattern.shape
    slots, block_len, _ = scf_blocks.shape
    tile = (block_len, panel.shape[1])
    count_cols = lax.axis_size("cols")
    owners = lax.axis_size("rows") * lax.axis_size("sub")
    chunk = br_dev // count_cols
    out = jax.ShapeDtypeStruct((br_dev, *tile), jnp.bfloat16)
    smem = pl.BlockSpec(memory_space=pltpu.SMEM)
    hbm = pl.BlockSpec(memory_space=pl.ANY)
    dma = pltpu.SemaphoreType.DMA
    one, two = pl.pallas_call(
        kernel,
        out_shape=(out, out),
        in_specs=[hbm, hbm, smem, smem],
        out_specs=(hbm, hbm),
        scratch_shapes=[
            pltpu.VMEM((slots, block_len, block_len), jnp.bfloat16),
            pltpu.VMEM((3 * br_dev, *tile), jnp.bfloat16),
            pltpu.VMEM((3 * br_dev, *tile), jnp.bfloat16),
            pltpu.VMEM((2, br_dev, *tile), SEND),
            pltpu.VMEM((2, count_cols, chunk, *tile), SEND),
            pltpu.VMEM((chunk, *tile), jnp.float32),
            pltpu.VMEM((br_dev, *tile), jnp.bfloat16),
            dma((4,)),
            dma((owners,)),
            dma((owners,)),
            dma((2,)),
            dma((2,)),
            dma((2, count_cols)),
            dma((2, count_cols)),
            dma((br_dev, 2)),
            dma((br_dev, 2)),
            dma((2, count_cols, chunk)),
            dma((2, count_cols, chunk)),
            dma((2, count_cols, chunk)),
            dma((2, count_cols, chunk)),
        ],
        compiler_params=pltpu.CompilerParams(
            collective_id=0, has_side_effects=True, vmem_limit_bytes=VMEM_MIB * 2**20
        ),
    )(scf_blocks, panel.reshape(br_dev, *tile), scf_source, pattern)
    return one.reshape(panel.shape), two.reshape(panel.shape)


def solution(mesh):
    return jax.shard_map(
        local,
        mesh=mesh,
        in_specs=(
            P(("groups", "rows", "cols", "sub"), None, None),
            P(("groups", "rows", "sub"), "cols"),
            P(("groups", "rows", "sub"), "cols"),
            P(("groups", "rows", "sub"), None),
        ),
        out_specs=(P(("groups", "rows", "sub"), None), P(("groups", "rows", "sub"), None)),
        check_vma=False,
    )
```

```python
import jax
import jax.numpy as jnp
from jax import lax
from jax.experimental import pallas as pl
from jax.experimental.pallas import tpu as pltpu
from jax.sharding import PartitionSpec as P

MESH = pl.DeviceIdType.MESH
SEND = jnp.bfloat16
VMEM_MIB = 57


def kernel(
    blocks_ref, panel_ref, order_ref, pattern_ref, one_ref, two_ref,
    recv, ext_one, ext_two, outbox, inbox, own, final,
    own_sem, block_send, block_recv, halo_send, halo_recv, pass_send, pass_recv,
    next_send, next_recv, sum_send, sum_recv, share_send, share_recv,
):
    slots = blocks_ref.shape[0]
    kb_col, br_dev = pattern_ref.shape
    count_sub = lax.axis_size("sub")
    count_cols = lax.axis_size("cols")
    owners = lax.axis_size("rows") * count_sub
    per_pair = slots // owners
    chunk = br_dev // count_cols
    tiles = owners * br_dev
    me = lax.axis_index("rows") * count_sub + lax.axis_index("sub")
    my_col = lax.axis_index("cols")
    right = (me + 1) % owners
    left = (me + owners - 1) % owners
    col_hops = range(1, count_cols)
    bases = (0, 2 * br_dev)

    def owner_id(owner):
        return {"rows": owner // count_sub, "sub": owner % count_sub}

    def col_id(hop):
        return {"cols": (my_col + hop) % count_cols}

    def remote(src, dst, send_sem, recv_sem, device_id):
        return pltpu.make_async_remote_copy(
            src_ref=src, dst_ref=dst, send_sem=send_sem, recv_sem=recv_sem,
            device_id=device_id, device_id_type=MESH,
        )

    barrier = pltpu.get_barrier_semaphore()

    def block_copy(target, slot):
        return remote(
            blocks_ref.at[pl.ds(target * per_pair, per_pair)],
            recv.at[pl.ds(me * per_pair, per_pair)],
            block_send.at[slot], block_recv.at[slot], owner_id(target),
        )

    middle = lax.axis_size("rows") // 2
    early = 2 * count_sub
    late = owners - early
    first_early = (middle - 1) * count_sub
    first_late = first_early + early
    my_row = lax.axis_index("rows")
    is_early = (my_row == middle) | (my_row == middle - 1)
    facing = 2 * middle - 1 - my_row

    def greet(owner):
        pl.semaphore_signal(barrier, inc=1, device_id=owner_id(owner), device_id_type=MESH)

    def greet_cols():
        for hop in col_hops:
            pl.semaphore_signal(barrier, inc=1, device_id=col_id(hop), device_id_type=MESH)

    @pl.when(is_early)
    def _():
        @pl.loop(1, early)
        def _(hop):
            greet(first_early + (me - first_early + hop) % early)

        greet_cols()
        pl.semaphore_wait(barrier, early - 1 + count_cols - 1)

        @pl.loop(0, count_sub)
        def _(step):
            half = owners // 2
            target = facing * count_sub + step
            block_copy(target, half + (target - me + owners) % half).start()

        @pl.loop(0, late)
        def _(step):
            greet((first_late + step) % owners)

        pl.semaphore_wait(barrier, late)

    @pl.when(jnp.logical_not(is_early))
    def _():
        place = (me + owners - first_late) % owners

        @pl.loop(1, late)
        def _(hop):
            greet((first_late + (place + hop) % late) % owners)

        greet_cols()
        pl.semaphore_wait(barrier, owners - 1 + count_cols - 1)

        @pl.loop(0, early)
        def _(step):
            greet(first_early + step)

    def halo_copy(side):
        return remote(
            panel_ref.at[pl.ds(my_col * chunk, chunk)],
            ext_one.at[pl.ds(bases[side] + my_col * chunk, chunk)],
            halo_send.at[side], halo_recv.at[side], owner_id((right, left)[side]),
        )

    def pass_copy(side, hop):
        part = ext_one.at[pl.ds(bases[side] + my_col * chunk, chunk)]
        return remote(part, part, pass_send.at[side, hop], pass_recv.at[side, hop], col_id(hop))

    own_blocks = pltpu.make_async_copy(
        blocks_ref.at[pl.ds(me * per_pair, per_pair)],
        recv.at[pl.ds(me * per_pair, per_pair)],
        own_sem.at[0],
    )
    own_panel = pltpu.make_async_copy(panel_ref, ext_one.at[pl.ds(br_dev, br_dev)], own_sem.at[1])

    for side in (0, 1):
        halo_copy(side).start()

    half = owners // 2
    while half:
        base = me // (2 * half) * (2 * half)
        sibling = base + (1 - (me - base) // half) * half

        @pl.loop(0, half)
        def _(step, half=half, sibling=sibling):
            target = sibling + (me + step) % half
            if half == owners // 2:
                @pl.when(jnp.logical_not(is_early & (target // count_sub == facing)))
                def _():
                    block_copy(target, half + step).start()
            else:
                block_copy(target, half + step).start()

        half //= 2

    own_blocks.start()
    own_panel.start()
    for side in (0, 1):
        halo_copy(side).wait()
        for hop in col_hops:
            pass_copy(side, hop).start()
    own_blocks.wait()
    own_panel.wait()
    for side in (0, 1):
        for hop in col_hops:
            pass_copy(side, hop).wait()

    @pl.loop(1, owners)
    def _(slot):
        block_copy((me + slot) % owners, slot).wait()

    first_tile = (me - 1) * br_dev

    def product(ext, row):
        lhs, rhs = [], []
        for k in range(kb_col):
            tile = pattern_ref[k, row] - first_tile
            tile = jnp.where(tile < 0, tile + tiles, tile)
            tile = jnp.where(tile >= tiles, tile - tiles, tile)
            tile = jnp.minimum(tile, 3 * br_dev - 1)
            lhs.append(recv[order_ref[k, row]])
            rhs.append(ext[tile])
        return jnp.dot(
            jnp.concatenate(lhs, axis=1), jnp.concatenate(rhs, axis=0),
            preferred_element_type=jnp.float32,
        )

    def sum_copy(turn, hop, step):
        row = (my_col + hop) % count_cols * chunk + step
        return remote(
            outbox.at[turn, row], inbox.at[turn, hop, step],
            sum_send.at[turn, hop, step], sum_recv.at[turn, hop, step], col_id(hop),
        )

    def multiply(ext, turn):
        for hop in col_hops:
            @pl.loop(0, chunk, unroll=chunk)
            def _(step, hop=hop):
                row = (my_col + hop) % count_cols * chunk + step
                outbox[turn, row] = product(ext, row).astype(SEND)
                sum_copy(turn, hop, step).start()

        @pl.loop(0, chunk, unroll=chunk)
        def _(step):
            own[step] = product(ext, my_col * chunk + step)

    def summed(turn, step):
        total = own[step]
        for hop in col_hops:
            sum_copy(turn, hop, step).wait()
            total = total + inbox[turn, hop, step].astype(jnp.float32)
        return total

    def share_copy(turn, ref, base, hop, step):
        part = ref.at[base + my_col * chunk + step]
        return remote(
            part, part, share_send.at[turn, hop, step], share_recv.at[turn, hop, step], col_id(hop)
        )

    def next_copy(row, side):
        return remote(
            ext_two.at[br_dev + row], ext_two.at[bases[side] + row],
            next_send.at[row, side], next_recv.at[row, side], owner_id((right, left)[side]),
        )

    multiply(ext_one, 0)

    @pl.loop(0, chunk)
    def _(step):
        row = my_col * chunk + step
        ext_two[br_dev + row] = summed(0, step).astype(jnp.bfloat16)
        for hop in col_hops:
            share_copy(0, ext_two, br_dev, hop, step).start()
        for side in (0, 1):
            next_copy(row, side).start()

    for hop in col_hops:
        @pl.loop(0, chunk)
        def _(step, hop=hop):
            share_copy(0, ext_two, br_dev, hop, step).wait()
            row = (my_col + count_cols - hop) % count_cols * chunk + step
            for side in (0, 1):
                next_copy(row, side).start()

    out_one = pltpu.make_async_copy(ext_two.at[pl.ds(br_dev, br_dev)], one_ref, own_sem.at[2])
    out_one.start()

    @pl.loop(0, br_dev)
    def _(row):
        for side in (0, 1):
            next_copy(row, side).wait()

    multiply(ext_two, 1)

    @pl.loop(0, chunk)
    def _(step):
        row = my_col * chunk + step
        total = 2.0 * summed(1, step) - ext_one[br_dev + row].astype(jnp.float32)
        final[row] = total.astype(jnp.bfloat16)
        for hop in col_hops:
            share_copy(1, final, 0, hop, step).start()

    for hop in col_hops:
        @pl.loop(0, chunk)
        def _(step, hop=hop):
            share_copy(1, final, 0, hop, step).wait()

    out_two = pltpu.make_async_copy(final, two_ref, own_sem.at[3])
    out_two.start()
    out_one.wait()
    out_two.wait()


def local(scf_blocks, scf_source, pattern, panel):
    br_dev, kb_col = pattern.shape
    slots, block_len, _ = scf_blocks.shape
    tile = (block_len, panel.shape[1])
    count_cols = lax.axis_size("cols")
    owners = lax.axis_size("rows") * lax.axis_size("sub")
    chunk = br_dev // count_cols
    out = jax.ShapeDtypeStruct((br_dev, *tile), jnp.bfloat16)
    smem = pl.BlockSpec(memory_space=pltpu.SMEM)
    hbm = pl.BlockSpec(memory_space=pl.ANY)
    dma = pltpu.SemaphoreType.DMA
    one, two = pl.pallas_call(
        kernel,
        out_shape=(out, out),
        in_specs=[hbm, hbm, smem, smem],
        out_specs=(hbm, hbm),
        scratch_shapes=[
            pltpu.VMEM((slots, block_len, block_len), jnp.bfloat16),
            pltpu.VMEM((3 * br_dev, *tile), jnp.bfloat16),
            pltpu.VMEM((3 * br_dev, *tile), jnp.bfloat16),
            pltpu.VMEM((2, br_dev, *tile), SEND),
            pltpu.VMEM((2, count_cols, chunk, *tile), SEND),
            pltpu.VMEM((chunk, *tile), jnp.float32),
            pltpu.VMEM((br_dev, *tile), jnp.bfloat16),
            dma((4,)),
            dma((owners,)),
            dma((owners,)),
            dma((2,)),
            dma((2,)),
            dma((2, count_cols)),
            dma((2, count_cols)),
            dma((br_dev, 2)),
            dma((br_dev, 2)),
            dma((2, count_cols, chunk)),
            dma((2, count_cols, chunk)),
            dma((2, count_cols, chunk)),
            dma((2, count_cols, chunk)),
        ],
        compiler_params=pltpu.CompilerParams(
            collective_id=0, has_side_effects=True, vmem_limit_bytes=VMEM_MIB * 2**20
        ),
    )(scf_blocks, panel.reshape(br_dev, *tile), scf_source.T, pattern.T)
    return one.reshape(panel.shape), two.reshape(panel.shape)


def solution(mesh):
    return jax.shard_map(
        local,
        mesh=mesh,
        in_specs=(
            P(("groups", "rows", "cols", "sub"), None, None),
            P(("groups", "rows", "sub"), "cols"),
            P(("groups", "rows", "sub"), "cols"),
            P(("groups", "rows", "sub"), None),
        ),
        out_specs=(P(("groups", "rows", "sub"), None), P(("groups", "rows", "sub"), None)),
        check_vma=False,
    )
```
